256 devices in a mesh: tp: 8 (over z), ep: 32 (over x, y, core).
Axes of the slice: x: 4, y: 4, z: 8, core: 2. Of those that a mesh axis runs over, the one named last changes fastest.
Arguments:
- tokens: bfloat16 [8192, 2048], P('ep'), may hold values from -6 to 6
- expert_ids: int32 [8192, 8], P('ep'), may hold values from 0 to 127, all different within a row; in each aligned block of 256 rows (0 to 255, 256 to 511, ...) at most 24 rows name the same one
- gate_weights: float32 [8192, 8], P('ep'), may hold values from 0.02 to 0.3
- grad_output: bfloat16 [8192, 2048], P('ep'), may hold values from -6 to 6
- w_gate_up: bfloat16 [256, 2048, 768], P(('tp', 'ep')), may hold values from -0.125 to 0.125
- w_down: bfloat16 [256, 384, 2048], P(('tp', 'ep')), may hold values from -0.21875 to 0.21875
Outputs:
- mixed: bfloat16 [8192, 2048], P('ep', 'tp')
- grad_tokens: bfloat16 [8192, 2048], P('ep', 'tp')
- grad_gates: float32 [8192, 8], P('ep', 'tp')
- grad_w_gate_up: bfloat16 [256, 2048, 768], P(('tp', 'ep'))
- grad_w_down: bfloat16 [256, 384, 2048], P(('tp', 'ep'))
The draws below stay inside these ranges and needn't reach their ends.
Inputs may be any that keep to these rules, and one draw needn't show every extreme that they name: `expert_ids`: each row names 8 different experts. Among the 256 rows of one index of ep no expert is named more than 24 times, and in every draw some expert is named exactly 24 times there.
All inputs are finite; a program needn't handle non-finite values.
Results may differ from the reference program's by a relative error of at most 0.012.
Values may be sent and summed in bfloat16 or wider, within the bound.
A program may use at most 128 MiB of HBM per device.

```python
import math
import jax
import jax.numpy as jnp
import numpy as np
from jax import lax

D = 2048
FF = 768
TOPK = 8
HALVES = 2
TOK_EP = 256
FF_PART = 384
EXPERTS = 128
CAP = 24
TOKENS = 8192


def level_of(own_key, dims, shards, low, high):
    def one(dim, parts):
        draws = jax.random.uniform(jax.random.fold_in(jax.random.fold_in(own_key, 6), dim), (parts,), jnp.float32, low / len(shards), high / len(shards))
        return jnp.repeat(jnp.exp(draws), dims[dim] // parts).reshape((-1,) + (1,) * (len(dims) - dim - 1))

    gain = one(*shards[0])
    for cut in shards[1:]:
        gain = gain * one(*cut)
    return gain


def routed_block(key, own, number, rows, count, top, most, slope):
    order = jax.random.permutation(key, count)
    heavy_load, common = portions_of(count, rows * top, most, slope, True), portions_of(count, rows * top, most, slope, False)
    places = jnp.arange(count)

    def named(lengths, offset_by):
        used = int((lengths > 0).sum())
        fixed = max(1, used // 4)
        passed = fixed + (places - fixed + offset_by * (used - fixed)) % max(1, count - fixed)
        return jnp.zeros((count,), jnp.int32).at[order[jnp.where(places < fixed, places, passed)]].set(jnp.asarray(lengths, jnp.int32))

    lengths = jnp.where(number % 4 == 0, named(heavy_load, number // 4), named(common, number - number // 4 - 1))
    mixed = jax.random.permutation(jax.random.fold_in(own, 3), count)
    donor, receiver = mixed[0:count // 2 * 2:2], mixed[1:count // 2 * 2:2]
    slack = jnp.minimum(lengths[donor] - 1, most - lengths[receiver]) // 2
    slack = jnp.where((donor == order[0]) | (receiver == order[0]) | (lengths[receiver] == 0), 0, jnp.maximum(slack, 0))
    passed = jax.random.randint(jax.random.fold_in(own, 4), (count // 2,), 0, 1 << 20) % (slack + 1)
    lengths = lengths.at[donor].add(-passed).at[receiver].add(passed)
    labels = jnp.searchsorted(jnp.cumsum(lengths), jnp.arange(rows * top), side="right").astype(jnp.int32)
    table = labels.reshape(top, rows).T
    table = table[jax.random.permutation(jax.random.fold_in(own, 1), rows)]
    offset_by = jax.random.randint(jax.random.fold_in(own, 2), (rows, 1), 0, top)
    return jnp.take_along_axis(table, (jnp.arange(top)[None, :] + offset_by) % top, axis=1)


def portions_of(number_of, total, bound, skew, full):
    portions = [(1 << 20) // math.isqrt(grade ** skew) + 1 for grade in range(1, number_of + 1)]
    largest = bound if full else min(bound, max(-(-total // number_of), total * portions[0] // sum(portions)))
    least = 1 if total - largest >= number_of - 1 else 0
    holding, spare = [largest] + [least] * (number_of - 1), total - largest - least * (number_of - 1)
    while spare > 0:
        candidates = [i for i in range(1, number_of) if holding[i] < largest] or [i for i in range(1, number_of) if holding[i] < bound]
        pool, remaining = sum([portions[i] for i in candidates]), spare
        for i in candidates:
            more = min(bound - holding[i], max(1, remaining * portions[i] // pool), spare)
            holding[i] = holding[i] + more
            spare = spare - more
    return np.array(holding)


def centred(rng, shape, scale, reach, shards=(), held_as=jnp.bfloat16):
    entries = jax.random.normal(rng, shape, jnp.float32) * scale
    if len(shards) > 0:
        entries = level_of(rng, shape, shards, -0.22, 0.18) * entries
    return jnp.clip(entries, min=-reach, max=reach).astype(held_as)


def setup_inputs(seed: int = 0) -> dict:
    streams_of = jax.random.split(jax.random.key(seed), 7)
    tokens = centred(streams_of[0], (TOKENS, D), 1.0, 6.0, ((0, 32),))
    expert_ids_keys = jax.random.split(jax.random.fold_in(streams_of[1], 1), TOKENS // TOK_EP)
    expert_ids_turns = jax.random.permutation(jax.random.fold_in(streams_of[1], 3), TOKENS // TOK_EP)
    expert_ids = jax.vmap(lambda own, number: routed_block(jax.random.fold_in(streams_of[1], 2), own, number, TOK_EP, EXPERTS, TOPK, CAP, 2))(expert_ids_keys, expert_ids_turns).reshape((TOKENS, TOPK))
    gate_weights = jnp.clip(0.02 + 0.28 * jax.random.uniform(streams_of[2], (TOKENS, TOPK), jnp.float32) ** level_of(streams_of[2], (TOKENS, TOPK), ((0, 32),), -0.2, 0.2), 0.02, 0.3)
    grad_output = centred(streams_of[3], (TOKENS, D), 1.0, 6.0, ((0, 32),))
    w_gate_up = centred(streams_of[4], (EXPERTS * HALVES, D, 2 * FF_PART), D ** -0.5, 0.125, ((0, 256),))
    w_down = centred(streams_of[5], (EXPERTS * HALVES, FF_PART, D), FF ** -0.5, 0.21875, ((0, 256),))
    return dict(tokens=tokens, expert_ids=expert_ids, gate_weights=gate_weights, grad_output=grad_output, w_gate_up=w_gate_up, w_down=w_down)


def expert_half(rows, scaled, gate_up, down):
    half_units = down.shape[0]
    pre = jnp.dot(rows, gate_up, preferred_element_type=jnp.float32)
    gate_pre = pre[:, :half_units]
    up_pre = pre[:, half_units:]
    sigma = jax.nn.sigmoid(gate_pre)
    active = (gate_pre * sigma * up_pre).astype(jnp.bfloat16)
    partial_out = jnp.dot(active, down, preferred_element_type=jnp.float32).astype(jnp.bfloat16)
    d_active = jnp.dot(scaled, down.T, preferred_element_type=jnp.float32)
    d_gate = d_active * up_pre * sigma * (1.0 + gate_pre * (1.0 - sigma))
    d_up = d_active * gate_pre * sigma
    d_pre = jnp.concatenate([d_gate, d_up], axis=1).astype(jnp.bfloat16)
    grad_down = jnp.dot(active.T, scaled, preferred_element_type=jnp.float32).astype(jnp.bfloat16)
    grad_gate_up = jnp.dot(rows.T, d_pre, preferred_element_type=jnp.float32).astype(jnp.bfloat16)
    input_part = jnp.dot(d_pre, gate_up.T, preferred_element_type=jnp.float32).astype(jnp.bfloat16)
    return partial_out, input_part, grad_gate_up, grad_down


def reference(tokens, expert_ids, gate_weights, grad_output, w_gate_up, w_down):
    total = tokens.shape[0]
    width = tokens.shape[1]
    blocks = total // TOK_EP
    assigned = TOK_EP * TOPK
    flat = expert_ids.reshape(blocks, assigned)
    onehot = (flat[:, :, None] == jnp.arange(EXPERTS, dtype=jnp.int32)[None, None, :]).astype(jnp.int32)
    earlier = jnp.cumsum(onehot, axis=1) - onehot
    slot = jnp.sum(earlier * onehot, axis=2).astype(jnp.int32)
    block_ids = jnp.arange(blocks, dtype=jnp.int32)[:, None]
    local = jnp.arange(assigned, dtype=jnp.int32)[None, :]
    position = (block_ids * CAP + slot).reshape(-1).astype(jnp.int32)
    token_index = (block_ids * TOK_EP + local // TOPK).reshape(-1).astype(jnp.int32)
    choice_index = jnp.broadcast_to(local % TOPK, (blocks, assigned)).reshape(-1).astype(jnp.int32)
    slots_all = blocks * CAP
    flat_ids = flat.reshape(-1).astype(jnp.int32)
    table_token = jnp.full((EXPERTS, slots_all), total, jnp.int32).at[flat_ids, position].set(token_index)
    table_choice = jnp.zeros((EXPERTS, slots_all), jnp.int32).at[flat_ids, position].set(choice_index)
    padded_tokens = jnp.concatenate([tokens, jnp.zeros((1, width), jnp.bfloat16)], axis=0)
    padded_grad = jnp.concatenate([grad_output, jnp.zeros((1, width), jnp.bfloat16)], axis=0)
    padded_gates = jnp.concatenate([gate_weights, jnp.zeros((1, TOPK), jnp.float32)], axis=0)

    def per_expert(carry, expert):
        mixed_sum, input_sum, gate_sum = carry
        index = table_token[expert]
        which = table_choice[expert]
        rows = padded_tokens[index]
        weight = padded_gates[index, which]
        grad_rows = padded_grad[index]
        scaled = (weight[:, None] * grad_rows.astype(jnp.float32)).astype(jnp.bfloat16)
        combined = jnp.zeros((index.shape[0], width), jnp.float32)
        input_rows = jnp.zeros((index.shape[0], width), jnp.float32)
        grads_gu = []
        grads_dn = []
        for half in range(HALVES):
            piece = (expert * HALVES + half).astype(jnp.int32)
            gate_up = lax.dynamic_index_in_dim(w_gate_up, piece, 0, keepdims=False)
            down = lax.dynamic_index_in_dim(w_down, piece, 0, keepdims=False)
            partial_out, input_part, grad_gu, grad_dn = expert_half(rows, scaled, gate_up, down)
            combined = combined + partial_out.astype(jnp.float32)
            input_rows = input_rows + input_part.astype(jnp.float32)
            grads_gu.append(grad_gu)
            grads_dn.append(grad_dn)
        combined = lax.optimization_barrier(combined.astype(jnp.bfloat16)).astype(jnp.float32)
        input_rows = lax.optimization_barrier(input_rows.astype(jnp.bfloat16)).astype(jnp.float32)
        mixed_sum = mixed_sum.at[index].add(weight[:, None] * combined, mode="drop")
        input_sum = input_sum.at[index].add(input_rows, mode="drop")
        gate_terms = jnp.sum(grad_rows.astype(jnp.float32) * combined, axis=1)
        gate_sum = gate_sum.at[index, which].add(gate_terms, mode="drop")
        return (mixed_sum, input_sum, gate_sum), (jnp.stack(grads_gu), jnp.stack(grads_dn))

    start = (jnp.zeros((total, width), jnp.float32), jnp.zeros((total, width), jnp.float32), jnp.zeros((total, TOPK), jnp.float32))
    final, stacked = lax.scan(per_expert, start, jnp.arange(EXPERTS, dtype=jnp.int32))
    mixed_sum, input_sum, gate_sum = final
    grad_w_gate_up = stacked[0].reshape(EXPERTS * HALVES, width, 2 * FF_PART)
    grad_w_down = stacked[1].reshape(EXPERTS * HALVES, FF_PART, width)
    return (mixed_sum.astype(jnp.bfloat16), input_sum.astype(jnp.bfloat16), gate_sum, grad_w_gate_up, grad_w_down)
```

```python
import functools

import jax
import jax.numpy as jnp
from jax import lax
from jax.experimental import pallas as pl
from jax.experimental.pallas import tpu as pltpu
from jax.sharding import PartitionSpec as P

MESH = pl.DeviceIdType.MESH
F32 = jnp.float32
BF16 = jnp.bfloat16
NX, NY, NC, NZ = 4, 4, 2, 8
OFFS = (1, 3, 2)
TOK, TOP, WIDTH, CAP, FFP = 256, 8, 2048, 24, 384
EXP = NX * NY
SLOTS = EXP * CAP
BLK = WIDTH // NZ
IN_CHUNKS = ((0, 512), (512, 512), (1024, 512), (1536, 512))
OUT_CHUNKS = ((0, 0, 5), (1, 0, 5), (0, 5, 3), (1, 5, 3))
NN = (((1,), (0,)), ((), ()))
NT = (((1,), (1,)), ((), ()))
TN = (((0,), (0,)), ((), ()))


def dot(a, b, dims=NN):
    return lax.dot_general(a, b, dims, preferred_element_type=F32)


def ring_step(pos):
    far = 3 - (pos - 1) // 2
    return jnp.where(pos == 0, 4, jnp.where(pos % 2 == 1, far, -far))


def kernel(
    tok, ids, gates, gout, wgu_in, wd_in,
    mixed_o, gtok_o, gg_o, gwgu_o, gwd_o,
    wgu, wd, send, mid, fin, rmid, rfin, rows2, act, dpre, pre, dact, onehot, comb,
    terms, zpart, zs, zr, gsend, gin, gst_gu, gst_d,
    w_ls, w_ss, w_rs, a_ss, a_rs, a_ls, p_ss, p_rs, z_ss, z_rs, g_ss, g_rs, o_s,
):
    z = lax.axis_index("tp")
    ep = lax.axis_index("ep")
    x, y, c = ep // (NY * NC), (ep // NC) % NY, ep % NC

    def dev(zz, xx, yy, cc):
        return (zz, (xx * NY + yy) * NC + cc)

    other = dev(z, x, y, 1 - c)
    own_rows = pl.multiple_of(c * SLOTS, SLOTS)

    def remote(src, dst, ss, rs, to):
        return pltpu.make_async_remote_copy(
            src_ref=src, dst_ref=dst, send_sem=ss, recv_sem=rs, device_id=to, device_id_type=MESH
        )

    w_local = [
        pltpu.make_async_copy(wgu_in.at[0], wgu.at[c], w_ls.at[0]),
        pltpu.make_async_copy(wd_in.at[0], wd.at[c], w_ls.at[1]),
    ]
    for cp in w_local:
        cp.start()
    w_out = [
        remote(wgu_in.at[0], wgu.at[c], w_ss.at[0], w_rs.at[0], other),
        remote(wd_in.at[0], wd.at[c], w_ss.at[1], w_rs.at[1], other),
    ]
    w_come = [
        remote(wgu_in.at[0], wgu.at[1 - c], w_ss.at[0], w_rs.at[0], other),
        remote(wd_in.at[0], wd.at[1 - c], w_ss.at[1], w_rs.at[1], other),
    ]

    barrier = pltpu.get_barrier_semaphore()
    peers = [dev(z, (x + d) % NX, y, c) for d in OFFS]
    peers += [dev(z, x, (y + d) % NY, c) for d in OFFS]
    peers += [dev((z + d) % NZ, x, y, c) for d in range(1, NZ)]
    peers += [other]
    for peer in peers:
        pl.semaphore_signal(barrier, inc=1, device_id=peer, device_id_type=MESH)

    local_ids = ids[...] - z * EXP
    hits, gate_rows = [], []
    for e in range(EXP):
        hit = jnp.where(local_ids == e, 1.0, 0.0)
        hits.append(jnp.sum(hit, axis=0, keepdims=True))
        gate_rows.append(jnp.sum(hit * gates[...], axis=0, keepdims=True))
    hit_all = jnp.concatenate(hits, axis=0)
    before = lax.broadcasted_iota(jnp.int32, (TOK, TOK), 0) < lax.broadcasted_iota(jnp.int32, (TOK, TOK), 1)
    rank = dot(hit_all.astype(BF16), jnp.where(before, 1.0, 0.0).astype(BF16))
    slot = lax.broadcasted_iota(jnp.int32, (CAP, TOK), 0).astype(F32)
    slot_gates = []
    for e in range(EXP):
        chosen = jnp.where(slot == rank[e : e + 1], hits[e], 0.0)
        onehot[e * CAP : (e + 1) * CAP, :] = chosen
        slot_gates.append(jnp.sum(chosen * gate_rows[e], axis=1, keepdims=True))
    slot_gate = jnp.concatenate(slot_gates, axis=0)
    picks = onehot[...].astype(BF16)

    def exchange(n, src, mid_ref, fin_ref, cols, x_first):
        col = slice(None) if cols is None else pl.ds(*cols)

        def part(ref, i, along_x):
            return ref.at[i, :, :, col] if along_x else ref.at[:, i, :, col]

        def phase(k, frm, into, along_x):
            here = x if along_x else y
            out, come = [], []
            for m, d in enumerate(OFFS):
                to, back = (here + d) % 4, (here + 4 - d) % 4
                place = dev(z, to, y, c) if along_x else dev(z, x, to, c)
                sems = (a_ss.at[n, k * 3 + m], a_rs.at[n, k * 3 + m])
                out.append(remote(part(frm, to, along_x), part(into, here, along_x), *sems, place))
                come.append(remote(part(frm, to, along_x), part(into, back, along_x), *sems, place))
            stay = pltpu.make_async_copy(part(frm, here, along_x), part(into, here, along_x), a_ls.at[n, k])
            return out, come, stay

        first = phase(0, src, mid_ref, x_first)
        second = phase(1, mid_ref, fin_ref, not x_first)

        def start(ph):
            for cp in ph[0]:
                cp.start()
            ph[2].start()

        def arrive(ph):
            for cp in ph[1]:
                cp.wait_recv()
            ph[2].wait()

        def forward():
            arrive(first)
            start(second)

        def sent(ph):
            for cp in ph[0]:
                cp.wait_send()

        return dict(
            start=lambda: start(first),
            forward=forward,
            arrive=lambda: arrive(second),
            sent1=lambda: sent(first),
            sent2=lambda: sent(second),
        )

    def stacked(value):
        return value.astype(F32).reshape(SLOTS, value.shape[-1]).astype(BF16)

    def unstacked(value):
        return value.reshape(NX, NY, CAP, value.shape[-1]).astype(BF16)

    incoming = []
    for n, cols in enumerate(IN_CHUNKS):
        incoming.append(
            [exchange(2 * n + a, send.at[a], mid.at[a], fin.at[a], cols, a == 0) for a in range(2)]
        )

    def gather(n):
        at, many = IN_CHUNKS[n]
        send[0, :, :, :, at : at + many] = unstacked(dot(picks, tok[:, at : at + many]))
        send[1, :, :, :, at : at + many] = unstacked(dot(picks, gout[:, at : at + many]) * slot_gate)

    def begin(n):
        for ex in incoming[n]:
            ex["start"]()

    def forward_in(n):
        for ex in incoming[n]:
            ex["forward"]()

    def first_part(n):
        at, many = IN_CHUNKS[n]
        for ex in incoming[n]:
            ex["arrive"]()
        for a in range(2):
            rows2[a, pl.ds(own_rows, SLOTS), at : at + many] = stacked(fin[a, :, :, :, at : at + many])

        def half(h, carry):
            new_pre = dot(rows2[0, pl.ds(own_rows, SLOTS), at : at + many], wgu[h, at : at + many, :])
            new_dact = dot(rows2[1, pl.ds(own_rows, SLOTS), at : at + many], wd[h, :, at : at + many], NT)
            if n > 0:
                new_pre = new_pre + pre[h]
                new_dact = new_dact + dact[h]
            if n < len(IN_CHUNKS) - 1:
                pre[h] = new_pre
                dact[h] = new_dact
            else:
                g, u = new_pre[:, :FFP], new_pre[:, FFP:]
                sigma = jax.nn.sigmoid(g)
                act[h, pl.ds(own_rows, SLOTS), :] = (g * sigma * u).astype(BF16)
                dpre[h, pl.ds(own_rows, SLOTS), :FFP] = (
                    new_dact * u * sigma * (1.0 + g * (1.0 - sigma))
                ).astype(BF16)
                dpre[h, pl.ds(own_rows, SLOTS), FFP:] = (new_dact * g * sigma).astype(BF16)
            return carry

        lax.fori_loop(0, 2, half, 0)

    gather(0)
    pl.semaphore_wait(barrier, len(peers))
    begin(0)
    for cp in w_out:
        cp.start()
    gather(1)
    begin(1)
    gather(2)
    forward_in(0)
    begin(2)
    gather(3)
    comb[1] = onehot[...].T.astype(BF16)
    comb[0] = (onehot[...] * slot_gate).T.astype(BF16)
    forward_in(1)
    begin(3)
    for cp in w_local:
        cp.wait()
    for cp in w_come:
        cp.wait_recv()
    forward_in(2)
    first_part(0)
    forward_in(3)
    first_part(1)
    first_part(2)
    for pair in incoming:
        for ex in pair:
            ex["sent1"]()
    first_part(3)

    pushes = [
        (rows2.at[0], own_rows),
        (rows2.at[1], own_rows),
        (act.at[1 - c], own_rows),
        (dpre.at[1 - c], own_rows),
    ]
    lands = [rows2.at[0], rows2.at[1], act.at[c], dpre.at[c]]
    their_rows = pl.multiple_of((1 - c) * SLOTS, SLOTS)
    push_out = [
        remote(r.at[pl.ds(at, SLOTS)], r.at[pl.ds(at, SLOTS)], p_ss.at[i], p_rs.at[i], other)
        for i, (r, at) in enumerate(pushes)
    ]
    push_come = [
        remote(r.at[pl.ds(their_rows, SLOTS)], r.at[pl.ds(their_rows, SLOTS)], p_ss.at[i], p_rs.at[i], other)
        for i, r in enumerate(lands)
    ]

    outgoing = []
    for n, (a, at, many) in enumerate(OUT_CHUNKS):
        half = many * BLK // 2
        base = 8 + 2 * n
        outgoing.append(
            [
                exchange(base + i, send.at[a], rmid.at[a], rfin.at[a], (at * BLK + i * half, half), i == 0)
                for i in range(2)
            ]
        )

    def plane_cols(pos):
        return pl.multiple_of(((z + ring_step(pos) + NZ) % NZ) * BLK, BLK)

    def second_part(n):
        a, at, many = OUT_CHUNKS[n]

        def block(pos, carry):
            j = plane_cols(pos)
            if a == 0:
                total = dot(act[0, pl.ds(own_rows, SLOTS), :], wd[0, :, pl.ds(j, BLK)])
                total += dot(act[1, pl.ds(own_rows, SLOTS), :], wd[1, :, pl.ds(j, BLK)])
            else:
                total = dot(dpre[0, pl.ds(own_rows, SLOTS), :], wgu[0, pl.ds(j, BLK), :], NT)
                total += dot(dpre[1, pl.ds(own_rows, SLOTS), :], wgu[1, pl.ds(j, BLK), :], NT)
            send[a, :, :, :, pl.ds(pl.multiple_of(pos * BLK, BLK), BLK)] = unstacked(total)
            return carry

        lax.fori_loop(at, at + many, block, 0)
        for ex in outgoing[n]:
            ex["start"]()

    def forward_out(n):
        for ex in outgoing[n]:
            ex["forward"]()

    def combine(n):
        a, at, many = OUT_CHUNKS[n]
        for ex in outgoing[n]:
            ex["arrive"]()

        def block(pos, carry):
            r = stacked(rfin[a, :, :, :, pl.ds(pl.multiple_of(pos * BLK, BLK), BLK)])
            zpart[a, pos] = dot(comb[a], r)
            if a == 0:
                terms[...] += dot(r, gout[:, pl.ds(plane_cols(pos), BLK)], NT)
            return carry

        lax.fori_loop(at, at + many, block, 0)

    ring_pos = (0, 1, 3, 5, 2, 4, 6)

    def ring_copy(a, m):
        to = dev((z + (1 if m < 4 else NZ - 1)) % NZ, x, y, c)
        return remote(zs.at[a, m], zr.at[a, m], z_ss.at[a, m], z_rs.at[a, m], to)

    def ring(a, m):
        total = zpart[a, ring_pos[m]]
        if m not in (0, 4):
            ring_copy(a, m - 1).wait_recv()
            total = total + zr[a, m - 1].astype(F32)
        zs[a, m] = total.astype(BF16)
        ring_copy(a, m).start()

    def ring_end(a, out):
        ring_copy(a, 3).wait_recv()
        ring_copy(a, 6).wait_recv()
        out[...] = (zpart[a, 7] + zr[a, 3].astype(F32) + zr[a, 6].astype(F32)).astype(BF16)

    out_copies = []

    def grad_gu(lo, hi):
        def tile(i, carry):
            cols = pl.ds(pl.multiple_of(i * 256, 256), 256)
            gst_gu[cols, :] = dot(rows2[0, :, cols], dpre[c], TN).astype(BF16)
            return carry

        lax.fori_loop(lo, hi, tile, 0)
        part = pl.ds(lo * 256, (hi - lo) * 256)
        cp = pltpu.make_async_copy(gst_gu.at[part], gwgu_o.at[0, part], o_s.at[len(out_copies)])
        cp.start()
        out_copies.append(cp)

    def grad_d(lo, hi):
        def tile(i, carry):
            cols = pl.ds(pl.multiple_of(i * 512, 512), 512)
            gst_d[:, cols] = dot(act[c], rows2[1, :, cols], TN).astype(BF16)
            return carry

        lax.fori_loop(lo, hi, tile, 0)
        part = pl.ds(lo * 512, (hi - lo) * 512)
        cp = pltpu.make_async_copy(gst_d.at[:, part], gwd_o.at[0, :, part], o_s.at[len(out_copies)])
        cp.start()
        out_copies.append(cp)

    second_part(0)
    second_part(1)
    for cp in push_out:
        cp.start()
    forward_out(0)
    second_part(2)
    second_part(3)
    terms[...] = jnp.zeros_like(terms)
    forward_out(1)
    for cp in push_come:
        cp.wait_recv()
    grad_gu(0, 2)
    combine(0)
    ring(0, 0)
    ring(0, 4)
    forward_out(2)
    grad_gu(2, 4)
    ring(0, 1)
    ring(0, 5)
    combine(1)
    ring(1, 0)
    ring(1, 4)
    ring(0, 2)
    forward_out(3)
    grad_gu(4, 6)
    ring(1, 1)
    ring(1, 5)
    grad_gu(6, 8)
    ring(1, 2)
    grad_d(0, 2)
    combine(2)
    ring(0, 3)
    ring(0, 6)

    kept = terms[...] * onehot[...]
    total = jnp.zeros((TOP, TOK), F32)
    for e in range(EXP):
        value = jnp.sum(kept[e * CAP : (e + 1) * CAP], axis=0, keepdims=True)
        total += jnp.where(local_ids == e, value, 0.0)
    for k in range(TOP):
        gsend[k] = jnp.broadcast_to(total[k : k + 1], (8, TOK))
    g_out, g_come = [], []
    for d in range(1, NZ):
        j, back = (z + d) % NZ, (z + NZ - d) % NZ
        sems = (g_ss.at[d - 1], g_rs.at[d - 1])
        g_out.append(remote(gsend.at[j], gin.at[z], *sems, dev(j, x, y, c)))
        g_come.append(remote(gsend.at[j], gin.at[back], *sems, dev(j, x, y, c)))
    for cp in g_out:
        cp.start()
    gin[z] = gsend[z]
    grad_d(2, 4)

    combine(3)
    ring(1, 3)
    ring(1, 6)
    ring_end(0, mixed_o)
    for cp in g_come:
        cp.wait_recv()
    gg_o[...] = jnp.sum(gin[...], axis=0)
    ring_end(1, gtok_o)

    for cp in w_out:
        cp.wait_send()
    for pair in incoming:
        for ex in pair:
            ex["sent2"]()
    for cp in push_out:
        cp.wait_send()
    for pair in outgoing:
        for ex in pair:
            ex["sent1"]()
            ex["sent2"]()
    for a in range(2):
        for m in range(7):
            ring_copy(a, m).wait_send()
    for cp in g_out:
        cp.wait_send()
    for cp in out_copies:
        cp.wait()


def local(tokens, expert_ids, gate_weights, grad_output, w_gate_up, w_down):
    vmem = pl.BlockSpec(memory_space=pltpu.VMEM)
    hbm = pl.BlockSpec(memory_space=pl.ANY)
    dma = pltpu.SemaphoreType.DMA
    quads = (2, NX, NY, CAP, WIDTH)
    mixed, grad_tokens, gates, grad_gu, grad_dn = pl.pallas_call(
        kernel,
        out_shape=(
            jax.ShapeDtypeStruct((TOK, BLK), BF16),
            jax.ShapeDtypeStruct((TOK, BLK), BF16),
            jax.ShapeDtypeStruct((8, TOK), F32),
            jax.ShapeDtypeStruct(w_gate_up.shape, BF16),
            jax.ShapeDtypeStruct(w_down.shape, BF16),
        ),
        in_specs=[vmem, vmem, vmem, vmem, hbm, hbm],
        out_specs=(vmem, vmem, vmem, hbm, hbm),
        scratch_shapes=[
            pltpu.VMEM((2, WIDTH, 2 * FFP), BF16),
            pltpu.VMEM((2, FFP, WIDTH), BF16),
            pltpu.VMEM(quads, BF16),
            pltpu.VMEM(quads, BF16),
            pltpu.VMEM(quads, BF16),
            pltpu.VMEM(quads, BF16),
            pltpu.VMEM(quads, BF16),
            pltpu.VMEM((2, NC * SLOTS, WIDTH), BF16),
            pltpu.VMEM((2, NC * SLOTS, FFP), BF16),
            pltpu.VMEM((2, NC * SLOTS, 2 * FFP), BF16),
            pltpu.VMEM((2, SLOTS, 2 * FFP), F32),
            pltpu.VMEM((2, SLOTS, FFP), F32),
            pltpu.VMEM((SLOTS, TOK), F32),
            pltpu.VMEM((2, TOK, SLOTS), BF16),
            pltpu.VMEM((SLOTS, TOK), F32),
            pltpu.VMEM((2, NZ, TOK, BLK), F32),
            pltpu.VMEM((2, 7, TOK, BLK), BF16),
            pltpu.VMEM((2, 7, TOK, BLK), BF16),
            pltpu.VMEM((TOP, 8, TOK), F32),
            pltpu.VMEM((NZ, 8, TOK), F32),
            pltpu.VMEM((WIDTH, 2 * FFP), BF16),
            pltpu.VMEM((FFP, WIDTH), BF16),
            dma((2,)), dma((2,)), dma((2,)),
            dma((16, 6)), dma((16, 6)), dma((16, 2)),
            dma((4,)), dma((4,)),
            dma((2, 7)), dma((2, 7)),
            dma((7,)), dma((7,)),
            dma((6,)),
        ],
        compiler_params=pltpu.CompilerParams(
            collective_id=0, has_side_effects=True, vmem_limit_bytes=63 * 1024 * 1024
        ),
        name="moe",
    )(tokens, expert_ids.T, gate_weights.T, grad_output, w_gate_up, w_down)
    return mixed, grad_tokens, gates[:1].T, grad_gu, grad_dn


def solution(mesh):
    placed = (
        P("ep", None),
        P("ep", None),
        P("ep", None),
        P("ep", None),
        P(("tp", "ep"), None, None),
        P(("tp", "ep"), None, None),
    )
    return jax.shard_map(
        local,
        mesh=mesh,
        in_specs=placed,
        out_specs=(
            P("ep", "tp"),
            P("ep", "tp"),
            P("ep", "tp"),
            P(("tp", "ep"), None, None),
            P(("tp", "ep"), None, None),
        ),
        check_vma=False,
    )
```

```python
import functools

import jax
import jax.numpy as jnp
from jax import lax
from jax.experimental import pallas as pl
from jax.experimental.pallas import tpu as pltpu
from jax.sharding import PartitionSpec as P

MESH = pl.DeviceIdType.MESH
F32 = jnp.float32
BF16 = jnp.bfloat16
NX, NY, NC, NZ = 4, 4, 2, 8
OFFS = (1, 3, 2)
TOK, TOP, WIDTH, CAP, FFP = 256, 8, 2048, 24, 384
EXP = NX * NY
SLOTS = EXP * CAP
BLK = WIDTH // NZ
PART = 512
IN_CHUNKS = ((0, 0), (0, 2 * PART), (1, 0), (1, 2 * PART))
BLK_FAR, BLK_MID, BLK_NEAR, BLK_OWN = (0, 3), (3, 5), (5, 7), (7, 8)
OUT_CHUNKS = tuple(
    ((a, lo * BLK, (hi - lo) * BLK // 2), (a, (lo + hi) * BLK // 2, (hi - lo) * BLK // 2))
    for lo, hi in (BLK_FAR, BLK_MID, BLK_NEAR)
    for a in (0, 1)
) + (((0, 7 * BLK, BLK), (1, 7 * BLK, BLK)),)
OUT_BLOCKS = tuple(((a, lo, hi),) for lo, hi in (BLK_FAR, BLK_MID, BLK_NEAR) for a in (0, 1)) + (
    ((0, 7, 8), (1, 7, 8)),
)
NN = (((1,), (0,)), ((), ()))
NT = (((1,), (1,)), ((), ()))
TN = (((0,), (0,)), ((), ()))


def dot(a, b, dims=NN):
    return lax.dot_general(a, b, dims, preferred_element_type=F32)


def ring_step(pos):
    far = 3 - (pos - 1) // 2
    return jnp.where(pos == 0, 4, jnp.where(pos % 2 == 1, far, -far))


def kernel(
    tok_in, ids, gates, gout_in, wgu_in, wd_in,
    mixed_o, gtok_o, gwgu_o, gwd_o, gg_o,
    tok, gout, wgu, wd, send, mid, fin, rmid, rfin, rows2, act, dpre, pre, dact, onehot, comb,
    terms, zpart, zs, zr, gsend, gin, gst_gu, gst_d,
    w_ls, w_ss, w_rs, a_ss, a_rs, a_ls, p_ss, p_rs, z_ss, z_rs, g_ss, g_rs, o_s,
):
    z = lax.axis_index("tp")
    ep = lax.axis_index("ep")
    x, y, c = ep // (NY * NC), (ep // NC) % NY, ep % NC

    def dev(zz, xx, yy, cc):
        return (zz, (xx * NY + yy) * NC + cc)

    other = dev(z, x, y, 1 - c)
    own_rows = pl.multiple_of(c * SLOTS, SLOTS)

    def remote(src, dst, ss, rs, to):
        return pltpu.make_async_remote_copy(
            src_ref=src, dst_ref=dst, send_sem=ss, recv_sem=rs, device_id=to, device_id_type=MESH
        )

    barrier = pltpu.get_barrier_semaphore()
    peers = [dev(z, (x + d) % NX, y, c) for d in OFFS]
    peers += [dev(z, x, (y + d) % NY, c) for d in OFFS]
    peers += [dev((z + d) % NZ, x, y, c) for d in range(1, NZ)]
    peers += [other]
    for peer in peers:
        pl.semaphore_signal(barrier, inc=1, device_id=peer, device_id_type=MESH)

    row_loads = [
        pltpu.make_async_copy(tok_in, tok, w_ls.at[2]),
        pltpu.make_async_copy(gout_in, gout, w_ls.at[3]),
    ]
    for cp in row_loads:
        cp.start()

    w_local = [
        pltpu.make_async_copy(wgu_in.at[0], wgu.at[c], w_ls.at[0]),
        pltpu.make_async_copy(wd_in.at[0], wd.at[c], w_ls.at[1]),
    ]
    for cp in w_local:
        cp.start()
    w_out = [
        remote(wgu_in.at[0], wgu.at[c], w_ss.at[0], w_rs.at[0], other),
        remote(wd_in.at[0], wd.at[c], w_ss.at[1], w_rs.at[1], other),
    ]
    w_come = [
        remote(wgu_in.at[0], wgu.at[1 - c], w_ss.at[0], w_rs.at[0], other),
        remote(wd_in.at[0], wd.at[1 - c], w_ss.at[1], w_rs.at[1], other),
    ]

    local_ids = ids[...] - z * EXP
    hits, gate_rows = [], []
    for e in range(EXP):
        hit = jnp.where(local_ids == e, 1.0, 0.0)
        hits.append(jnp.sum(hit, axis=0, keepdims=True))
        gate_rows.append(jnp.sum(hit * gates[...], axis=0, keepdims=True))
    hit_all = jnp.concatenate(hits, axis=0)
    before = lax.broadcasted_iota(jnp.int32, (TOK, TOK), 0) < lax.broadcasted_iota(jnp.int32, (TOK, TOK), 1)
    rank = dot(hit_all.astype(BF16), jnp.where(before, 1.0, 0.0).astype(BF16))
    slot = lax.broadcasted_iota(jnp.int32, (CAP, TOK), 0).astype(F32)
    slot_gates = []
    for e in range(EXP):
        chosen = jnp.where(slot == rank[e : e + 1], hits[e], 0.0)
        onehot[e * CAP : (e + 1) * CAP, :] = chosen
        slot_gates.append(jnp.sum(chosen * gate_rows[e], axis=1, keepdims=True))
    slot_gate = jnp.concatenate(slot_gates, axis=0)
    picks = onehot[...].astype(BF16)

    def exchange(n, src, mid_ref, fin_ref, cols, x_first):
        col = slice(None) if cols is None else pl.ds(*cols)

        def part(ref, i, along_x):
            return ref.at[i, :, :, col] if along_x else ref.at[:, i, :, col]

        def phase(k, frm, into, along_x):
            here = x if along_x else y
            out, come = [], []
            for m, d in enumerate(OFFS):
                to, back = (here + d) % 4, (here + 4 - d) % 4
                place = dev(z, to, y, c) if along_x else dev(z, x, to, c)
                sems = (a_ss.at[n, k * 3 + m], a_rs.at[n, k * 3 + m])
                out.append(remote(part(frm, to, along_x), part(into, here, along_x), *sems, place))
                come.append(remote(part(frm, to, along_x), part(into, back, along_x), *sems, place))
            stay = pltpu.make_async_copy(part(frm, here, along_x), part(into, here, along_x), a_ls.at[n, k])
            return out, come, stay

        first = phase(0, src, mid_ref, x_first)
        second = phase(1, mid_ref, fin_ref, not x_first)

        def start(ph):
            for cp in ph[0]:
                cp.start()
            ph[2].start()

        def arrive(ph):
            for cp in ph[1]:
                cp.wait_recv()
            ph[2].wait()

        def forward():
            arrive(first)
            start(second)

        def sent(ph):
            for cp in ph[0]:
                cp.wait_send()

        return dict(
            start=lambda: start(first),
            forward=forward,
            arrive=lambda: arrive(second),
            sent1=lambda: sent(first),
            sent2=lambda: sent(second),
        )

    def stacked(value):
        return value.astype(F32).reshape(SLOTS, value.shape[-1]).astype(BF16)

    def unstacked(value):
        return value.reshape(NX, NY, CAP, value.shape[-1]).astype(BF16)

    incoming = []
    for n, (a, at) in enumerate(IN_CHUNKS):
        incoming.append(
            [
                exchange(2 * n + i, send.at[a], mid.at[a], fin.at[a], (at + i * PART, PART), i == 0)
                for i in range(2)
            ]
        )

    def gather(n):
        a, at = IN_CHUNKS[n]
        cols = slice(at, at + 2 * PART)
        if a == 0:
            send[a, :, :, :, cols] = unstacked(dot(picks, tok[:, cols]))
        else:
            send[a, :, :, :, cols] = unstacked(dot(picks, gout[:, cols]) * slot_gate)

    def begin(n):
        for ex in incoming[n]:
            ex["start"]()

    def forward_in(n):
        for ex in incoming[n]:
            ex["forward"]()

    def first_part(n):
        a, at = IN_CHUNKS[n]
        cols = slice(at, at + 2 * PART)
        for i, ex in enumerate(incoming[n]):
            ex["arrive"]()
            piece = slice(at + i * PART, at + (i + 1) * PART)
            rows2[a, pl.ds(own_rows, SLOTS), piece] = stacked(fin[a, :, :, :, piece])

        def half(h, carry):
            rows = rows2[a, pl.ds(own_rows, SLOTS), cols]
            if a == 0:
                total = dot(rows, wgu[h, cols, :])
                if at == 0:
                    pre[h] = total
                else:
                    total = total + pre[h]
                    pre[h] = total
                    g, u = total[:, :FFP], total[:, FFP:]
                    act[h, pl.ds(own_rows, SLOTS), :] = (g * jax.nn.sigmoid(g) * u).astype(BF16)
            else:
                total = dot(rows, wd[h, :, cols], NT)
                if at == 0:
                    dact[h] = total
                else:
                    total = total + dact[h]
                    g, u = pre[h, :, :FFP], pre[h, :, FFP:]
                    sigma = jax.nn.sigmoid(g)
                    dpre[h, pl.ds(own_rows, SLOTS), :FFP] = (
                        total * u * sigma * (1.0 + g * (1.0 - sigma))
                    ).astype(BF16)
                    dpre[h, pl.ds(own_rows, SLOTS), FFP:] = (total * g * sigma).astype(BF16)
            return carry

        lax.fori_loop(0, 2, half, 0)

    row_loads[0].wait()
    gather(0)
    pl.semaphore_wait(barrier, len(peers))
    begin(0)
    for cp in w_out:
        cp.start()
    gather(1)
    begin(1)
    row_loads[1].wait()
    gather(2)
    forward_in(0)
    begin(2)
    gather(3)
    forward_in(1)
    begin(3)
    comb[1] = onehot[...].T.astype(BF16)
    comb[0] = (onehot[...] * slot_gate).T.astype(BF16)
    for cp in w_local:
        cp.wait()
    for cp in w_come:
        cp.wait_recv()
    first_part(0)
    forward_in(2)
    for pair in incoming[:2]:
        for ex in pair:
            ex["sent1"]()
    first_part(1)

    pushes = [
        (rows2.at[0], own_rows),
        (rows2.at[1], own_rows),
        (act.at[1 - c], own_rows),
        (dpre.at[1 - c], own_rows),
    ]
    lands = [rows2.at[0], rows2.at[1], act.at[c], dpre.at[c]]
    their_rows = pl.multiple_of((1 - c) * SLOTS, SLOTS)
    push_out = [
        remote(r.at[pl.ds(at, SLOTS)], r.at[pl.ds(at, SLOTS)], p_ss.at[i], p_rs.at[i], other)
        for i, (r, at) in enumerate(pushes)
    ]
    push_come = [
        remote(r.at[pl.ds(their_rows, SLOTS)], r.at[pl.ds(their_rows, SLOTS)], p_ss.at[i], p_rs.at[i], other)
        for i, r in enumerate(lands)
    ]

    outgoing = []
    for n, halves in enumerate(OUT_CHUNKS):
        outgoing.append(
            [
                exchange(8 + 2 * n + i, send.at[a], rmid.at[a], rfin.at[a], (at, many), i == 0)
                for i, (a, at, many) in enumerate(halves)
            ]
        )

    def plane_cols(pos):
        return pl.multiple_of(((z + ring_step(pos) + NZ) % NZ) * BLK, BLK)

    def second_part(n):
        for a, lo, hi in OUT_BLOCKS[n]:

            def block(pos, carry):
                j = plane_cols(pos)
                if a == 0:
                    total = dot(act[0, pl.ds(own_rows, SLOTS), :], wd[0, :, pl.ds(j, BLK)])
                    total += dot(act[1, pl.ds(own_rows, SLOTS), :], wd[1, :, pl.ds(j, BLK)])
                else:
                    total = dot(dpre[0, pl.ds(own_rows, SLOTS), :], wgu[0, pl.ds(j, BLK), :], NT)
                    total += dot(dpre[1, pl.ds(own_rows, SLOTS), :], wgu[1, pl.ds(j, BLK), :], NT)
                send[a, :, :, :, pl.ds(pl.multiple_of(pos * BLK, BLK), BLK)] = unstacked(total)
                return carry

            lax.fori_loop(lo, hi, block, 0)
        for ex in outgoing[n]:
            ex["start"]()

    def forward_out(n):
        for ex in outgoing[n]:
            ex["forward"]()

    def block_sum(a, pos):
        r = stacked(rfin[a, :, :, :, pl.ds(pl.multiple_of(pos * BLK, BLK), BLK)])
        zpart[a, pos] = dot(comb[a], r)
        if a == 0:
            terms[...] += dot(r, gout[:, pl.ds(plane_cols(pos), BLK)], NT)

    def combine(n):
        for ex in outgoing[n]:
            ex["arrive"]()
        for a, lo, hi in OUT_BLOCKS[n]:

            def block(pos, carry):
                block_sum(a, pos)
                return carry

            lax.fori_loop(lo, hi, block, 0)

    ring_pos = ((0, 1, 3, 5, 2, 4, 6), (0, 2, 4, 6, 1, 3, 5))

    def ring_copy(a, m):
        to = dev((z + (1 if (m < 4) == (a == 0) else NZ - 1)) % NZ, x, y, c)
        return remote(zs.at[a, m], zr.at[a, m], z_ss.at[a, m], z_rs.at[a, m], to)

    def ring(a, m):
        total = zpart[a, ring_pos[a][m]]
        if m not in (0, 4):
            ring_copy(a, m - 1).wait_recv()
            total = total + zr[a, m - 1].astype(F32)
        zs[a, m] = total.astype(BF16)
        ring_copy(a, m).start()

    def ring_end(a, out):
        ring_copy(a, 3).wait_recv()
        ring_copy(a, 6).wait_recv()
        out[...] = (zpart[a, 7] + zr[a, 3].astype(F32) + zr[a, 6].astype(F32)).astype(BF16)

    out_copies = []

    def grad_gu(lo, hi):
        def tile(i, carry):
            cols = pl.ds(pl.multiple_of(i * 256, 256), 256)
            gst_gu[cols, :] = dot(rows2[0, :, cols], dpre[c], TN).astype(BF16)
            return carry

        lax.fori_loop(lo, hi, tile, 0)
        part = pl.ds(lo * 256, (hi - lo) * 256)
        cp = pltpu.make_async_copy(gst_gu.at[part], gwgu_o.at[0, part], o_s.at[len(out_copies)])
        cp.start()
        out_copies.append(cp)

    def grad_d(lo, hi):
        def tile(i, carry):
            cols = pl.ds(pl.multiple_of(i * 512, 512), 512)
            gst_d[:, cols] = dot(act[c], rows2[1, :, cols], TN).astype(BF16)
            return carry

        lax.fori_loop(lo, hi, tile, 0)
        part = pl.ds(lo * 512, (hi - lo) * 512)
        cp = pltpu.make_async_copy(gst_d.at[:, part], gwd_o.at[0, :, part], o_s.at[len(out_copies)])
        cp.start()
        out_copies.append(cp)

    second_part(0)
    forward_in(3)
    terms[...] = jnp.zeros_like(terms)
    first_part(2)
    for pair in incoming[2:]:
        for ex in pair:
            ex["sent1"]()
    forward_out(0)
    first_part(3)
    second_part(1)
    for cp in push_out:
        cp.start()
    second_part(2)
    combine(0)
    ring(0, 0)
    ring(0, 4)
    forward_out(1)
    second_part(3)
    forward_out(2)
    second_part(4)
    ring(0, 1)
    combine(1)
    ring(1, 0)
    ring(1, 4)
    forward_out(3)
    second_part(5)
    combine(2)
    ring(0, 2)
    ring(0, 5)
    forward_out(4)
    second_part(6)
    ring(1, 1)
    for cp in push_come:
        cp.wait_recv()
    grad_gu(0, 2)
    combine(3)
    ring(1, 2)
    ring(1, 5)
    forward_out(5)
    grad_gu(2, 4)
    combine(4)
    ring(0, 3)
    ring(0, 6)
    forward_out(6)

    grad_gu(4, 6)
    combine(5)
    ring(1, 3)
    ring(1, 6)
    grad_gu(6, 8)
    grad_d(0, 4)
    combine(6)

    kept = terms[...] * onehot[...]
    total = jnp.zeros((TOP, TOK), F32)
    for e in range(EXP):
        value = jnp.sum(kept[e * CAP : (e + 1) * CAP], axis=0, keepdims=True)
        total += jnp.where(local_ids == e, value, 0.0)
    for k in range(TOP):
        gsend[k] = jnp.broadcast_to(total[k : k + 1], (8, TOK))
    g_out, g_come = [], []
    for d in range(1, NZ):
        j, back = (z + d) % NZ, (z + NZ - d) % NZ
        sems = (g_ss.at[d - 1], g_rs.at[d - 1])
        g_out.append(remote(gsend.at[j], gin.at[z], *sems, dev(j, x, y, c)))
        g_come.append(remote(gsend.at[j], gin.at[back], *sems, dev(j, x, y, c)))
    for cp in g_out:
        cp.start()
    gin[z] = gsend[z]

    ring_end(0, mixed_o)
    ring_end(1, gtok_o)
    for cp in g_come:
        cp.wait_recv()
    gg_o[...] = jnp.sum(gin[...], axis=0)[:1]

    for cp in w_out:
        cp.wait_send()
    for pair in incoming:
        for ex in pair:
            ex["sent2"]()
    for cp in push_out:
        cp.wait_send()
    for pair in outgoing:
        for ex in pair:
            ex["sent1"]()
            ex["sent2"]()
    for a in range(2):
        for m in range(7):
            ring_copy(a, m).wait_send()
    for cp in g_out:
        cp.wait_send()
    for cp in out_copies:
        cp.wait()


def move(m_in, t_in, gu_in, d_in, g_in, m_out, t_out, gu_out, d_out, g_out, m, t, gu, d, sems):
    trips = []
    for src, via, dst, pieces in (
        (gu_in.at[0], gu, gu_out.at[0], 8),
        (d_in.at[0], d, d_out.at[0], 4),
        (m_in, m, m_out, 1),
        (t_in, t, t_out, 1),
    ):
        many = via.shape[0] // pieces
        for i in range(pieces):
            n, at = len(trips), pl.ds(i * many, many)
            trips.append(
                (
                    pltpu.make_async_copy(src.at[at], via.at[at], sems.at[n, 0]),
                    pltpu.make_async_copy(via.at[at], dst.at[at], sems.at[n, 1]),
                )
            )
    for come, _ in trips:
        come.start()
    for come, leave in trips:
        come.wait()
        leave.start()
    g_out[...] = g_in[...]
    for _, leave in trips:
        leave.wait()


def local(tokens, expert_ids, gate_weights, grad_output, w_gate_up, w_down):
    vmem = pl.BlockSpec(memory_space=pltpu.VMEM)
    hbm = pl.BlockSpec(memory_space=pl.ANY)
    dma = pltpu.SemaphoreType.DMA
    quads = (2, NX, NY, CAP, WIDTH)
    results = pl.pallas_call(
        kernel,
        out_shape=(
            jax.ShapeDtypeStruct((TOK, BLK), BF16),
            jax.ShapeDtypeStruct((TOK, BLK), BF16),
            jax.ShapeDtypeStruct(w_gate_up.shape, BF16),
            jax.ShapeDtypeStruct(w_down.shape, BF16),
            jax.ShapeDtypeStruct((1, TOK), F32),
        ),
        in_specs=[hbm, vmem, vmem, hbm, hbm, hbm],
        out_specs=(vmem, vmem, hbm, hbm, vmem),
        scratch_shapes=[
            pltpu.VMEM((TOK, WIDTH), BF16),
            pltpu.VMEM((TOK, WIDTH), BF16),
            pltpu.VMEM((2, WIDTH, 2 * FFP), BF16),
            pltpu.VMEM((2, FFP, WIDTH), BF16),
            pltpu.VMEM(quads, BF16),
            pltpu.VMEM(quads, BF16),
            pltpu.VMEM(quads, BF16),
            pltpu.VMEM(quads, BF16),
            pltpu.VMEM(quads, BF16),
            pltpu.VMEM((2, NC * SLOTS, WIDTH), BF16),
            pltpu.VMEM((2, NC * SLOTS, FFP), BF16),
            pltpu.VMEM((2, NC * SLOTS, 2 * FFP), BF16),
            pltpu.VMEM((2, SLOTS, 2 * FFP), F32),
            pltpu.VMEM((2, SLOTS, FFP), F32),
            pltpu.VMEM((SLOTS, TOK), F32),
            pltpu.VMEM((2, TOK, SLOTS), BF16),
            pltpu.VMEM((SLOTS, TOK), F32),
            pltpu.VMEM((2, NZ, TOK, BLK), F32),
            pltpu.VMEM((2, 7, TOK, BLK), BF16),
            pltpu.VMEM((2, 7, TOK, BLK), BF16),
            pltpu.VMEM((TOP, 8, TOK), F32),
            pltpu.VMEM((NZ, 8, TOK), F32),
            pltpu.VMEM((WIDTH, 2 * FFP), BF16),
            pltpu.VMEM((FFP, WIDTH), BF16),
            dma((4,)), dma((2,)), dma((2,)),
            dma((22, 6)), dma((22, 6)), dma((22, 2)),
            dma((4,)), dma((4,)),
            dma((2, 7)), dma((2, 7)),
            dma((7,)), dma((7,)),
            dma((6,)),
        ],
        compiler_params=pltpu.CompilerParams(
            collective_id=0, has_side_effects=True, vmem_limit_bytes=63 * 1024 * 1024
        ),
        name="moe",
    )(tokens, expert_ids.T, gate_weights.T, grad_output, w_gate_up, w_down)
    mixed, grad_tokens, grad_gu, grad_dn, gates = pl.pallas_call(
        move,
        out_shape=tuple(jax.ShapeDtypeStruct(r.shape, r.dtype) for r in results),
        in_specs=[hbm] * 4 + [vmem],
        out_specs=(hbm,) * 4 + (vmem,),
        scratch_shapes=[
            pltpu.VMEM((TOK, BLK), BF16),
            pltpu.VMEM((TOK, BLK), BF16),
            pltpu.VMEM((WIDTH, 2 * FFP), BF16),
            pltpu.VMEM((FFP, WIDTH), BF16),
            dma((14, 2)),
        ],
        compiler_params=pltpu.CompilerParams(vmem_limit_bytes=63 * 1024 * 1024),
        name="move",
    )(*results)
    return mixed, grad_tokens, gates.T, grad_gu, grad_dn


def solution(mesh):
    placed = (
        P("ep", None),
        P("ep", None),
        P("ep", None),
        P("ep", None),
        P(("tp", "ep"), None, None),
        P(("tp", "ep"), None, None),
    )
    return jax.shard_map(
        local,
        mesh=mesh,
        in_specs=placed,
        out_specs=(
            P("ep", "tp"),
            P("ep", "tp"),
            P("ep", "tp"),
            P(("tp", "ep"), None, None),
            P(("tp", "ep"), None, None),
        ),
        check_vma=False,
    )
```

```python
import functools

import jax
import jax.numpy as jnp
from jax import lax
from jax.experimental import pallas as pl
from jax.experimental.pallas import tpu as pltpu
from jax.sharding import PartitionSpec as P

MESH = pl.DeviceIdType.MESH
F32 = jnp.float32
BF16 = jnp.bfloat16
NX, NY, NC, NZ = 4, 4, 2, 8
OFFS = (1, 3, 2)
TOK, TOP, WIDTH, CAP, FFP = 256, 8, 2048, 24, 384
EXP = NX * NY
SLOTS = EXP * CAP
BLK = WIDTH // NZ
PART = 512
IN_CHUNKS = ((0, 0), (0, 2 * PART), (1, 0), (1, 2 * PART))
OUT_BLOCKS = ((0, 0, 5), (1, 0, 3), (0, 5, 8), (1, 3, 5), (1, 5, 8))
OUT_CHUNKS = tuple(
    ((a, lo * BLK, (hi - lo) * BLK // 2), (a, (lo + hi) * BLK // 2, (hi - lo) * BLK // 2)) for a, lo, hi in OUT_BLOCKS
)
PIECES = 2
NN = (((1,), (0,)), ((), ()))
NT = (((1,), (1,)), ((), ()))
TN = (((0,), (0,)), ((), ()))


def dot(a, b, dims=NN):
    return lax.dot_general(a, b, dims, preferred_element_type=F32)


def ring_step(pos):
    far = 3 - (pos - 1) // 2
    return jnp.where(pos == 0, 4, jnp.where(pos % 2 == 1, far, -far))


def kernel(
    tok_in, ids, gates, gout_in, wgu_in, wd_in,
    mixed_o, gtok_o, gwgu_o, gwd_o, gg_o,
    tok, gout, wgu, wd, send, mid, fin, rmid, rfin, rows2, act, dpre, pre, dact, onehot, comb,
    terms, zpart, zs, zr, gsend, gin,
    w_ls, w_ss, w_rs, a_ss, a_rs, a_ls, p_ss, p_rs, z_ss, z_rs, g_ss, g_rs,
):
    z = lax.axis_index("tp")
    ep = lax.axis_index("ep")
    x, y, c = ep // (NY * NC), (ep // NC) % NY, ep % NC

    def dev(zz, xx, yy, cc):
        return (zz, (xx * NY + yy) * NC + cc)

    other = dev(z, x, y, 1 - c)
    own_rows = pl.multiple_of(c * SLOTS, SLOTS)

    def remote(src, dst, ss, rs, to):
        return pltpu.make_async_remote_copy(
            src_ref=src, dst_ref=dst, send_sem=ss, recv_sem=rs, device_id=to, device_id_type=MESH
        )

    barrier = pltpu.get_barrier_semaphore()
    peers = [dev(z, (x + d) % NX, y, c) for d in OFFS]
    peers += [dev(z, x, (y + d) % NY, c) for d in OFFS]
    peers += [dev((z + d) % NZ, x, y, c) for d in range(1, NZ)]
    peers += [other]
    for peer in peers:
        pl.semaphore_signal(barrier, inc=1, device_id=peer, device_id_type=MESH)

    row_loads = [
        pltpu.make_async_copy(tok_in, tok, w_ls.at[2]),
        pltpu.make_async_copy(gout_in, gout, w_ls.at[3]),
    ]
    for cp in row_loads:
        cp.start()

    w_local = [
        pltpu.make_async_copy(wgu_in.at[0], wgu.at[c], w_ls.at[0]),
        pltpu.make_async_copy(wd_in.at[0], wd.at[c], w_ls.at[1]),
    ]
    for cp in w_local:
        cp.start()
    w_out = [
        remote(wgu_in.at[0], wgu.at[c], w_ss.at[0], w_rs.at[0], other),
        remote(wd_in.at[0], wd.at[c], w_ss.at[1], w_rs.at[1], other),
    ]
    w_come = [
        remote(wgu_in.at[0], wgu.at[1 - c], w_ss.at[0], w_rs.at[0], other),
        remote(wd_in.at[0], wd.at[1 - c], w_ss.at[1], w_rs.at[1], other),
    ]

    local_ids = ids[...] - z * EXP
    hits, gate_rows = [], []
    for e in range(EXP):
        hit = jnp.where(local_ids == e, 1.0, 0.0)
        hits.append(jnp.sum(hit, axis=0, keepdims=True))
        gate_rows.append(jnp.sum(hit * gates[...], axis=0, keepdims=True))
    hit_all = jnp.concatenate(hits, axis=0)
    before = lax.broadcasted_iota(jnp.int32, (TOK, TOK), 0) < lax.broadcasted_iota(jnp.int32, (TOK, TOK), 1)
    rank = dot(hit_all.astype(BF16), jnp.where(before, 1.0, 0.0).astype(BF16))
    slot = lax.broadcasted_iota(jnp.int32, (CAP, TOK), 0).astype(F32)
    slot_gates = []
    for e in range(EXP):
        chosen = jnp.where(slot == rank[e : e + 1], hits[e], 0.0)
        onehot[e * CAP : (e + 1) * CAP, :] = chosen
        slot_gates.append(jnp.sum(chosen * gate_rows[e], axis=1, keepdims=True))
    slot_gate = jnp.concatenate(slot_gates, axis=0)
    picks = onehot[...].astype(BF16)

    def exchange(n, src, mid_ref, fin_ref, cols, x_first):
        col = slice(None) if cols is None else pl.ds(*cols)

        def part(ref, i, along_x):
            return ref.at[i, :, :, col] if along_x else ref.at[:, i, :, col]

        def phase(k, frm, into, along_x):
            here = x if along_x else y
            out, come = [], []
            for m, d in enumerate(OFFS):
                to, back = (here + d) % 4, (here + 4 - d) % 4
                place = dev(z, to, y, c) if along_x else dev(z, x, to, c)
                sems = (a_ss.at[n, k * 3 + m], a_rs.at[n, k * 3 + m])
                out.append(remote(part(frm, to, along_x), part(into, here, along_x), *sems, place))
                come.append(remote(part(frm, to, along_x), part(into, back, along_x), *sems, place))
            stay = pltpu.make_async_copy(part(frm, here, along_x), part(into, here, along_x), a_ls.at[n, k])
            return out, come, stay

        first = phase(0, src, mid_ref, x_first)
        second = phase(1, mid_ref, fin_ref, not x_first)

        def start(ph):
            for cp in ph[0]:
                cp.start()
            ph[2].start()

        def arrive(ph):
            for cp in ph[1]:
                cp.wait_recv()
            ph[2].wait()

        def forward():
            arrive(first)
            start(second)

        def sent(ph):
            for cp in ph[0]:
                cp.wait_send()

        return dict(
            start=lambda: start(first),
            forward=forward,
            arrive=lambda: arrive(second),
            sent1=lambda: sent(first),
            sent2=lambda: sent(second),
        )

    def stacked(value):
        return value.astype(F32).reshape(SLOTS, value.shape[-1]).astype(BF16)

    def unstacked(value):
        return value.reshape(NX, NY, CAP, value.shape[-1]).astype(BF16)

    incoming = []
    for n, (a, at) in enumerate(IN_CHUNKS):
        incoming.append(
            [
                exchange(2 * n + i, send.at[a], mid.at[a], fin.at[a], (at + i * PART, PART), i == 0)
                for i in range(2)
            ]
        )

    def gather(n):
        a, at = IN_CHUNKS[n]
        cols = slice(at, at + 2 * PART)
        if a == 0:
            send[a, :, :, :, cols] = unstacked(dot(picks, tok[:, cols]))
        else:
            send[a, :, :, :, cols] = unstacked(dot(picks, gout[:, cols]) * slot_gate)

    def begin(n):
        for ex in incoming[n]:
            ex["start"]()

    def forward_in(n):
        for ex in incoming[n]:
            ex["forward"]()

    def first_part(n):
        a, at = IN_CHUNKS[n]
        cols = slice(at, at + 2 * PART)
        for i, ex in enumerate(incoming[n]):
            ex["arrive"]()
            piece = slice(at + i * PART, at + (i + 1) * PART)
            rows2[a, pl.ds(own_rows, SLOTS), piece] = stacked(fin[a, :, :, :, piece])

        def half(h, carry):
            rows = rows2[a, pl.ds(own_rows, SLOTS), cols]
            if a == 0:
                total = dot(rows, wgu[h, cols, :])
                if at == 0:
                    pre[h] = total
                else:
                    total = total + pre[h]
                    pre[h] = total
                    g, u = total[:, :FFP], total[:, FFP:]
                    act[h, pl.ds(own_rows, SLOTS), :] = (g * jax.nn.sigmoid(g) * u).astype(BF16)
            else:
                total = dot(rows, wd[h, :, cols], NT)
                if at == 0:
                    dact[h] = total
                else:
                    total = total + dact[h]
                    g, u = pre[h, :, :FFP], pre[h, :, FFP:]
                    sigma = jax.nn.sigmoid(g)
                    dpre[h, pl.ds(own_rows, SLOTS), :FFP] = (
                        total * u * sigma * (1.0 + g * (1.0 - sigma))
                    ).astype(BF16)
                    dpre[h, pl.ds(own_rows, SLOTS), FFP:] = (total * g * sigma).astype(BF16)
            return carry

        lax.fori_loop(0, 2, half, 0)

    row_loads[0].wait()
    gather(0)
    pl.semaphore_wait(barrier, len(peers))
    begin(0)
    for cp in w_out:
        cp.start()
    gather(1)
    begin(1)
    row_loads[1].wait()
    gather(2)
    forward_in(0)
    begin(2)
    gather(3)
    forward_in(1)
    begin(3)
    comb[1] = onehot[...].T.astype(BF16)
    comb[0] = (onehot[...] * slot_gate).T.astype(BF16)
    for cp in w_local:
        cp.wait()
    for cp in w_come:
        cp.wait_recv()
    first_part(0)
    forward_in(2)
    for pair in incoming[:2]:
        for ex in pair:
            ex["sent1"]()
    forward_in(3)
    first_part(1)

    pushes = [
        (rows2.at[0], own_rows),
        (rows2.at[1], own_rows),
        (act.at[1 - c], own_rows),
        (dpre.at[1 - c], own_rows),
    ]
    lands = [rows2.at[0], rows2.at[1], act.at[c], dpre.at[c]]
    their_rows = pl.multiple_of((1 - c) * SLOTS, SLOTS)
    push_out = [
        remote(r.at[pl.ds(at, SLOTS)], r.at[pl.ds(at, SLOTS)], p_ss.at[i], p_rs.at[i], other)
        for i, (r, at) in enumerate(pushes)
    ]
    push_come = [
        remote(r.at[pl.ds(their_rows, SLOTS)], r.at[pl.ds(their_rows, SLOTS)], p_ss.at[i], p_rs.at[i], other)
        for i, r in enumerate(lands)
    ]

    outgoing = []
    for n, halves in enumerate(OUT_CHUNKS):
        outgoing.append(
            [
                exchange(8 + 2 * n + i, send.at[a], rmid.at[a], rfin.at[a], (at, many), i == 0)
                for i, (a, at, many) in enumerate(halves)
            ]
        )

    def plane_cols(pos):
        return pl.multiple_of(((z + ring_step(pos) + NZ) % NZ) * BLK, BLK)

    def second_part(n):
        a, lo, hi = OUT_BLOCKS[n]

        def block(pos, carry):
            j = plane_cols(pos)
            if a == 0:
                total = dot(act[0, pl.ds(own_rows, SLOTS), :], wd[0, :, pl.ds(j, BLK)])
                total += dot(act[1, pl.ds(own_rows, SLOTS), :], wd[1, :, pl.ds(j, BLK)])
            else:
                total = dot(dpre[0, pl.ds(own_rows, SLOTS), :], wgu[0, pl.ds(j, BLK), :], NT)
                total += dot(dpre[1, pl.ds(own_rows, SLOTS), :], wgu[1, pl.ds(j, BLK), :], NT)
            send[a, :, :, :, pl.ds(pl.multiple_of(pos * BLK, BLK), BLK)] = unstacked(total)
            return carry

        lax.fori_loop(lo, hi, block, 0)

    def start_out(n):
        for ex in outgoing[n]:
            ex["start"]()

    def forward_out(n):
        for ex in outgoing[n]:
            ex["forward"]()

    def block_sum(a, pos):
        r = stacked(rfin[a, :, :, :, pl.ds(pl.multiple_of(pos * BLK, BLK), BLK)])
        zpart[a, pos] = dot(comb[a], r)
        if a == 0:
            terms[...] += dot(r, gout[:, pl.ds(plane_cols(pos), BLK)], NT)

    def arrive_out(n):
        for ex in outgoing[n]:
            ex["arrive"]()

    def combine(n):
        a, lo, hi = OUT_BLOCKS[n]
        arrive_out(n)

        def block(pos, carry):
            block_sum(a, pos)
            return carry

        lax.fori_loop(lo, hi, block, 0)

    ring_pos = ((0, 1, 3, 5, 2, 4, 6), (0, 2, 4, 6, 1, 3, 5))

    def ring_copy(a, m, piece):
        to = dev((z + (1 if (m < 4) == (a == 0) else NZ - 1)) % NZ, x, y, c)
        rows = pl.ds(piece * (TOK // PIECES), TOK // PIECES)
        sems = (z_ss.at[a, m, piece], z_rs.at[a, m, piece])
        return remote(zs.at[a, m, rows], zr.at[a, m, rows], *sems, to)

    def ring(a, m):
        for piece in range(PIECES):
            rows = slice(piece * (TOK // PIECES), (piece + 1) * (TOK // PIECES))
            total = zpart[a, ring_pos[a][m], rows]
            if m not in (0, 4):
                ring_copy(a, m - 1, piece).wait_recv()
                total = total + zr[a, m - 1, rows].astype(F32)
            zs[a, m, rows] = total.astype(BF16)
            ring_copy(a, m, piece).start()

    def ring_end(a, out):
        for piece in range(PIECES):
            ring_copy(a, 3, piece).wait_recv()
            ring_copy(a, 6, piece).wait_recv()
        out[...] = (zpart[a, 7] + zr[a, 3].astype(F32) + zr[a, 6].astype(F32)).astype(BF16)

    def grad_gu(lo, hi):
        def tile(i, carry):
            cols = pl.ds(pl.multiple_of(i * 256, 256), 256)
            gwgu_o[0, cols, :] = dot(rows2[0, :, cols], dpre[c], TN).astype(BF16)
            return carry

        lax.fori_loop(lo, hi, tile, 0)

    def grad_d(lo, hi):
        def tile(i, carry):
            cols = pl.ds(pl.multiple_of(i * 512, 512), 512)
            gwd_o[0, :, cols] = dot(act[c], rows2[1, :, cols], TN).astype(BF16)
            return carry

        lax.fori_loop(lo, hi, tile, 0)

    second_part(0)
    start_out(0)
    terms[...] = jnp.zeros_like(terms)
    first_part(2)
    second_part(2)
    start_out(2)
    forward_out(0)
    for pair in incoming[2:]:
        for ex in pair:
            ex["sent1"]()
    first_part(3)
    second_part(1)
    start_out(1)
    forward_out(2)
    for cp in push_out:
        cp.start()
    combine(0)
    ring(0, 0)
    ring(0, 4)
    second_part(3)
    forward_out(1)
    start_out(3)
    second_part(4)
    start_out(4)
    ring(0, 1)
    ring(0, 5)
    combine(2)
    forward_out(3)
    combine(1)
    ring(1, 0)
    ring(1, 4)
    ring(0, 2)
    forward_out(4)
    for cp in push_come:
        cp.wait_recv()
    grad_gu(0, 2)
    ring(1, 1)
    ring(0, 6)
    ring(0, 3)
    grad_gu(2, 3)
    combine(3)
    ring(1, 2)
    ring(1, 5)
    grad_gu(3, 5)
    kept = terms[...] * onehot[...]
    total = jnp.zeros((TOP, TOK), F32)
    for e in range(EXP):
        value = jnp.sum(kept[e * CAP : (e + 1) * CAP], axis=0, keepdims=True)
        total += jnp.where(local_ids == e, value, 0.0)
    for k in range(TOP):
        gsend[k] = jnp.broadcast_to(total[k : k + 1], (8, TOK))
    g_out, g_come = [], []
    for d in range(1, NZ):
        j, back = (z + d) % NZ, (z + NZ - d) % NZ
        sems = (g_ss.at[d - 1], g_rs.at[d - 1])
        g_out.append(remote(gsend.at[j], gin.at[z], *sems, dev(j, x, y, c)))
        g_come.append(remote(gsend.at[j], gin.at[back], *sems, dev(j, x, y, c)))
    for cp in g_out:
        cp.start()
    gin[z] = gsend[z]

    grad_gu(5, 8)
    arrive_out(4)
    block_sum(1, 5)
    ring(1, 6)
    block_sum(1, 6)
    ring(1, 3)
    block_sum(1, 7)
    grad_d(0, 4)
    ring_end(0, mixed_o)
    for cp in g_come:
        cp.wait_recv()
    gg_o[...] = jnp.sum(gin[...], axis=0)[:1]
    ring_end(1, gtok_o)

    for cp in w_out:
        cp.wait_send()
    for pair in incoming:
        for ex in pair:
            ex["sent2"]()
    for cp in push_out:
        cp.wait_send()
    for pair in outgoing:
        for ex in pair:
            ex["sent1"]()
            ex["sent2"]()
    for a in range(2):
        for m in range(7):
            for piece in range(PIECES):
                ring_copy(a, m, piece).wait_send()
    for cp in g_out:
        cp.wait_send()


def move(m_in, t_in, gu_in, d_in, g_in, m_out, t_out, gu_out, d_out, g_out, sems):
    copies = []
    for src, dst, pieces in (
        (gu_in.at[0], gu_out.at[0], 4),
        (d_in.at[0], d_out.at[0], 2),
        (m_in, m_out, 1),
        (t_in, t_out, 1),
        (g_in, g_out, 1),
    ):
        many = src.shape[0] // pieces
        for i in range(pieces):
            at = pl.ds(i * many, many)
            copies.append(pltpu.make_async_copy(src.at[at], dst.at[at], sems.at[len(copies)]))
    for cp in copies:
        cp.start()
    for cp in copies:
        cp.wait()


def local(tokens, expert_ids, gate_weights, grad_output, w_gate_up, w_down):
    vmem = pl.BlockSpec(memory_space=pltpu.VMEM)
    hbm = pl.BlockSpec(memory_space=pl.ANY)
    dma = pltpu.SemaphoreType.DMA
    quads = (2, NX, NY, CAP, WIDTH)
    results = pl.pallas_call(
        kernel,
        out_shape=(
            pltpu.VMEM((TOK, BLK), BF16),
            pltpu.VMEM((TOK, BLK), BF16),
            pltpu.VMEM(w_gate_up.shape, BF16),
            pltpu.VMEM(w_down.shape, BF16),
            pltpu.VMEM((1, TOK), F32),
        ),
        in_specs=[hbm, vmem, vmem, hbm, hbm, hbm],
        out_specs=(vmem,) * 5,
        scratch_shapes=[
            pltpu.VMEM((TOK, WIDTH), BF16),
            pltpu.VMEM((TOK, WIDTH), BF16),
            pltpu.VMEM((2, WIDTH, 2 * FFP), BF16),
            pltpu.VMEM((2, FFP, WIDTH), BF16),
            pltpu.VMEM(quads, BF16),
            pltpu.VMEM(quads, BF16),
            pltpu.VMEM(quads, BF16),
            pltpu.VMEM(quads, BF16),
            pltpu.VMEM(quads, BF16),
            pltpu.VMEM((2, NC * SLOTS, WIDTH), BF16),
            pltpu.VMEM((2, NC * SLOTS, FFP), BF16),
            pltpu.VMEM((2, NC * SLOTS, 2 * FFP), BF16),
            pltpu.VMEM((2, SLOTS, 2 * FFP), F32),
            pltpu.VMEM((2, SLOTS, FFP), F32),
            pltpu.VMEM((SLOTS, TOK), F32),
            pltpu.VMEM((2, TOK, SLOTS), BF16),
            pltpu.VMEM((SLOTS, TOK), F32),
            pltpu.VMEM((2, NZ, TOK, BLK), F32),
            pltpu.VMEM((2, 7, TOK, BLK), BF16),
            pltpu.VMEM((2, 7, TOK, BLK), BF16),
            pltpu.VMEM((TOP, 8, TOK), F32),
            pltpu.VMEM((NZ, 8, TOK), F32),
            dma((4,)), dma((2,)), dma((2,)),
            dma((18, 6)), dma((18, 6)), dma((18, 2)),
            dma((4,)), dma((4,)),
            dma((2, 7, PIECES)), dma((2, 7, PIECES)),
            dma((7,)), dma((7,)),
        ],
        compiler_params=pltpu.CompilerParams(
            collective_id=0, has_side_effects=True, vmem_limit_bytes=54 * 1024 * 1024
        ),
        name="moe",
    )(tokens, expert_ids.T, gate_weights.T, grad_output, w_gate_up, w_down)
    mixed, grad_tokens, grad_gu, grad_dn, gates = pl.pallas_call(
        move,
        out_shape=tuple(jax.ShapeDtypeStruct(r.shape, r.dtype) for r in results),
        in_specs=[hbm] * 5,
        out_specs=(hbm,) * 5,
        scratch_shapes=[dma((9,))],
        compiler_params=pltpu.CompilerParams(vmem_limit_bytes=2 * 1024 * 1024),
        name="move",
    )(*results)
    return mixed, grad_tokens, gates.T, grad_gu, grad_dn


def solution(mesh):
    placed = (
        P("ep", None),
        P("ep", None),
        P("ep", None),
        P("ep", None),
        P(("tp", "ep"), None, None),
        P(("tp", "ep"), None, None),
    )
    return jax.shard_map(
        local,
        mesh=mesh,
        in_specs=placed,
        out_specs=(
            P("ep", "tp"),
            P("ep", "tp"),
            P("ep", "tp"),
            P(("tp", "ep"), None, None),
            P(("tp", "ep"), None, None),
        ),
        check_vma=False,
    )
```

```python
import functools

import jax
import jax.numpy as jnp
from jax import lax
from jax.experimental import pallas as pl
from jax.experimental.pallas import tpu as pltpu
from jax.sharding import PartitionSpec as P

MESH = pl.DeviceIdType.MESH
F32 = jnp.float32
BF16 = jnp.bfloat16
NX, NY, NC, NZ = 4, 4, 2, 8
OFFS = (1, 3, 2)
TOK, TOP, WIDTH, CAP, FFP = 256, 8, 2048, 24, 384
EXP = NX * NY
SLOTS = EXP * CAP
BLK = WIDTH // NZ
PART = 512
IN_CHUNKS = ((0, 0), (0, 2 * PART), (1, 0), (1, 2 * PART))
OUT_BLOCKS = ((0, 0, 5), (1, 0, 3), (0, 5, 8), (1, 3, 5), (1, 5, 8))
OUT_CHUNKS = tuple(
    ((a, lo * BLK, (hi - lo) * BLK // 2), (a, (lo + hi) * BLK // 2, (hi - lo) * BLK // 2)) for a, lo, hi in OUT_BLOCKS
)
PIECES = 2
NN = (((1,), (0,)), ((), ()))
NT = (((1,), (1,)), ((), ()))
TN = (((0,), (0,)), ((), ()))


def dot(a, b, dims=NN):
    return lax.dot_general(a, b, dims, preferred_element_type=F32)


def ring_step(pos):
    far = 3 - (pos - 1) // 2
    return jnp.where(pos == 0, 4, jnp.where(pos % 2 == 1, far, -far))


def kernel(
    tok_in, ids, gates, gout_in, wgu_in, wd_in,
    mixed_o, gtok_o, gwgu_o, gwd_o, gg_o,
    tok, gout, wgu, wd, send, mid, fin, rmid, rfin, rows2, act, dpre, pre, dact, onehot, comb,
    terms, zpart, zs, zr, gsend, gin,
    w_ls, w_ss, w_rs, a_ss, a_rs, a_ls, p_ss, p_rs, z_ss, z_rs, g_ss, g_rs,
):
    z = lax.axis_index("tp")
    ep = lax.axis_index("ep")
    x, y, c = ep // (NY * NC), (ep // NC) % NY, ep % NC

    def dev(zz, xx, yy, cc):
        return (zz, (xx * NY + yy) * NC + cc)

    other = dev(z, x, y, 1 - c)
    own_rows = pl.multiple_of(c * SLOTS, SLOTS)

    def remote(src, dst, ss, rs, to):
        return pltpu.make_async_remote_copy(
            src_ref=src, dst_ref=dst, send_sem=ss, recv_sem=rs, device_id=to, device_id_type=MESH
        )

    barrier = pltpu.get_barrier_semaphore()
    peers = [dev(z, (x + d) % NX, y, c) for d in OFFS]
    peers += [dev(z, x, (y + d) % NY, c) for d in OFFS]
    peers += [dev((z + d) % NZ, x, y, c) for d in range(1, NZ)]
    peers += [other]
    for peer in peers:
        pl.semaphore_signal(barrier, inc=1, device_id=peer, device_id_type=MESH)

    row_loads = [
        pltpu.make_async_copy(tok_in, tok, w_ls.at[2]),
        pltpu.make_async_copy(gout_in, gout, w_ls.at[3]),
    ]
    for cp in row_loads:
        cp.start()

    w_local = [
        pltpu.make_async_copy(wgu_in.at[0], wgu.at[c], w_ls.at[0]),
        pltpu.make_async_copy(wd_in.at[0], wd.at[c], w_ls.at[1]),
    ]
    for cp in w_local:
        cp.start()
    w_out = [
        remote(wgu_in.at[0], wgu.at[c], w_ss.at[0], w_rs.at[0], other),
        remote(wd_in.at[0], wd.at[c], w_ss.at[1], w_rs.at[1], other),
    ]
    w_come = [
        remote(wgu_in.at[0], wgu.at[1 - c], w_ss.at[0], w_rs.at[0], other),
        remote(wd_in.at[0], wd.at[1 - c], w_ss.at[1], w_rs.at[1], other),
    ]

    local_ids = ids[...] - z * EXP
    hits, gate_rows = [], []
    for e in range(EXP):
        hit = jnp.where(local_ids == e, 1.0, 0.0)
        hits.append(jnp.sum(hit, axis=0, keepdims=True))
        gate_rows.append(jnp.sum(hit * gates[...], axis=0, keepdims=True))
    hit_all = jnp.concatenate(hits, axis=0)
    before = lax.broadcasted_iota(jnp.int32, (TOK, TOK), 0) < lax.broadcasted_iota(jnp.int32, (TOK, TOK), 1)
    rank = dot(hit_all.astype(BF16), jnp.where(before, 1.0, 0.0).astype(BF16))
    slot = lax.broadcasted_iota(jnp.int32, (CAP, TOK), 0).astype(F32)
    slot_gates = []
    for e in range(EXP):
        chosen = jnp.where(slot == rank[e : e + 1], hits[e], 0.0)
        onehot[e * CAP : (e + 1) * CAP, :] = chosen
        slot_gates.append(jnp.sum(chosen * gate_rows[e], axis=1, keepdims=True))
    slot_gate = jnp.concatenate(slot_gates, axis=0)
    picks = onehot[...].astype(BF16)

    def exchange(n, src, mid_ref, fin_ref, cols, x_first):
        col = slice(None) if cols is None else pl.ds(*cols)

        def part(ref, i, along_x):
            return ref.at[i, :, :, col] if along_x else ref.at[:, i, :, col]

        def phase(k, frm, into, along_x):
            here = x if along_x else y
            out, come = [], []
            for m, d in enumerate(OFFS):
                to, back = (here + d) % 4, (here + 4 - d) % 4
                place = dev(z, to, y, c) if along_x else dev(z, x, to, c)
                sems = (a_ss.at[n, k * 3 + m], a_rs.at[n, k * 3 + m])
                out.append(remote(part(frm, to, along_x), part(into, here, along_x), *sems, place))
                come.append(remote(part(frm, to, along_x), part(into, back, along_x), *sems, place))
            stay = pltpu.make_async_copy(part(frm, here, along_x), part(into, here, along_x), a_ls.at[n, k])
            return out, come, stay

        first = phase(0, src, mid_ref, x_first)
        second = phase(1, mid_ref, fin_ref, not x_first)

        def start(ph):
            for cp in ph[0]:
                cp.start()
            ph[2].start()

        def arrive(ph):
            for cp in ph[1]:
                cp.wait_recv()
            ph[2].wait()

        def forward():
            arrive(first)
            start(second)

        def sent(ph):
            for cp in ph[0]:
                cp.wait_send()

        return dict(
            start=lambda: start(first),
            forward=forward,
            arrive=lambda: arrive(second),
            sent1=lambda: sent(first),
            sent2=lambda: sent(second),
        )

    def stacked(value):
        return value.astype(F32).reshape(SLOTS, value.shape[-1]).astype(BF16)

    def unstacked(value):
        return value.reshape(NX, NY, CAP, value.shape[-1]).astype(BF16)

    incoming = []
    for n, (a, at) in enumerate(IN_CHUNKS):
        incoming.append(
            [
                exchange(2 * n + i, send.at[a], mid.at[a], fin.at[a], (at + i * PART, PART), i == 0)
                for i in range(2)
            ]
        )

    def gather(n):
        a, at = IN_CHUNKS[n]
        cols = slice(at, at + 2 * PART)
        if a == 0:
            send[a, :, :, :, cols] = unstacked(dot(picks, tok[:, cols]))
        else:
            send[a, :, :, :, cols] = unstacked(dot(picks, gout[:, cols]) * slot_gate)

    def begin(n):
        for ex in incoming[n]:
            ex["start"]()

    def forward_in(n):
        for ex in incoming[n]:
            ex["forward"]()

    def first_part(n):
        a, at = IN_CHUNKS[n]
        cols = slice(at, at + 2 * PART)
        for i, ex in enumerate(incoming[n]):
            ex["arrive"]()
            piece = slice(at + i * PART, at + (i + 1) * PART)
            rows2[a, pl.ds(own_rows, SLOTS), piece] = stacked(fin[a, :, :, :, piece])

        def half(h, carry):
            rows = rows2[a, pl.ds(own_rows, SLOTS), cols]
            if a == 0:
                total = dot(rows, wgu[h, cols, :])
                if at == 0:
                    pre[h] = total
                else:
                    total = total + pre[h]
                    pre[h] = total
                    g, u = total[:, :FFP], total[:, FFP:]
                    act[h, pl.ds(own_rows, SLOTS), :] = (g * jax.nn.sigmoid(g) * u).astype(BF16)
            else:
                total = dot(rows, wd[h, :, cols], NT)
                if at == 0:
                    dact[h] = total
                else:
                    total = total + dact[h]
                    g, u = pre[h, :, :FFP], pre[h, :, FFP:]
                    sigma = jax.nn.sigmoid(g)
                    dpre[h, pl.ds(own_rows, SLOTS), :FFP] = (
                        total * u * sigma * (1.0 + g * (1.0 - sigma))
                    ).astype(BF16)
                    dpre[h, pl.ds(own_rows, SLOTS), FFP:] = (total * g * sigma).astype(BF16)
            return carry

        lax.fori_loop(0, 2, half, 0)

    row_loads[0].wait()
    gather(0)
    pl.semaphore_wait(barrier, len(peers))
    begin(0)
    for cp in w_out:
        cp.start()
    gather(1)
    begin(1)
    row_loads[1].wait()
    gather(2)
    begin(2)
    forward_in(0)
    gather(3)
    forward_in(1)
    begin(3)
    comb[1] = onehot[...].T.astype(BF16)
    comb[0] = (onehot[...] * slot_gate).T.astype(BF16)
    for cp in w_local:
        cp.wait()
    for cp in w_come:
        cp.wait_recv()
    first_part(0)
    forward_in(2)
    for pair in incoming[:2]:
        for ex in pair:
            ex["sent1"]()
    forward_in(3)
    first_part(1)

    pushes = [
        (rows2.at[0], own_rows),
        (rows2.at[1], own_rows),
        (act.at[1 - c], own_rows),
        (dpre.at[1 - c], own_rows),
    ]
    lands = [rows2.at[0], rows2.at[1], act.at[c], dpre.at[c]]
    their_rows = pl.multiple_of((1 - c) * SLOTS, SLOTS)
    push_out = [
        remote(r.at[pl.ds(at, SLOTS)], r.at[pl.ds(at, SLOTS)], p_ss.at[i], p_rs.at[i], other)
        for i, (r, at) in enumerate(pushes)
    ]
    push_come = [
        remote(r.at[pl.ds(their_rows, SLOTS)], r.at[pl.ds(their_rows, SLOTS)], p_ss.at[i], p_rs.at[i], other)
        for i, r in enumerate(lands)
    ]

    outgoing = []
    for n, halves in enumerate(OUT_CHUNKS):
        outgoing.append(
            [
                exchange(8 + 2 * n + i, send.at[a], rmid.at[a], rfin.at[a], (at, many), i == 0)
                for i, (a, at, many) in enumerate(halves)
            ]
        )

    def plane_cols(pos):
        return pl.multiple_of(((z + ring_step(pos) + NZ) % NZ) * BLK, BLK)

    def second_part(n):
        a, lo, hi = OUT_BLOCKS[n]

        def block(pos, carry):
            j = plane_cols(pos)
            if a == 0:
                total = dot(act[0, pl.ds(own_rows, SLOTS), :], wd[0, :, pl.ds(j, BLK)])
                total += dot(act[1, pl.ds(own_rows, SLOTS), :], wd[1, :, pl.ds(j, BLK)])
            else:
                total = dot(dpre[0, pl.ds(own_rows, SLOTS), :], wgu[0, pl.ds(j, BLK), :], NT)
                total += dot(dpre[1, pl.ds(own_rows, SLOTS), :], wgu[1, pl.ds(j, BLK), :], NT)
            send[a, :, :, :, pl.ds(pl.multiple_of(pos * BLK, BLK), BLK)] = unstacked(total)
            return carry

        lax.fori_loop(lo, hi, block, 0)

    def start_out(n):
        for ex in outgoing[n]:
            ex["start"]()

    def forward_out(n):
        for ex in outgoing[n]:
            ex["forward"]()

    def block_sum(a, pos):
        r = stacked(rfin[a, :, :, :, pl.ds(pl.multiple_of(pos * BLK, BLK), BLK)])
        zpart[a, pos] = dot(comb[a], r)
        if a == 0:
            terms[...] += dot(r, gout[:, pl.ds(plane_cols(pos), BLK)], NT)

    def arrive_out(n):
        for ex in outgoing[n]:
            ex["arrive"]()

    def combine(n):
        a, lo, hi = OUT_BLOCKS[n]
        arrive_out(n)

        def block(pos, carry):
            block_sum(a, pos)
            return carry

        lax.fori_loop(lo, hi, block, 0)

    ring_pos = ((0, 1, 3, 5, 2, 4, 6), (0, 2, 4, 6, 1, 3, 5))

    def ring_copy(a, m, piece):
        to = dev((z + (1 if (m < 4) == (a == 0) else NZ - 1)) % NZ, x, y, c)
        rows = pl.ds(piece * (TOK // PIECES), TOK // PIECES)
        sems = (z_ss.at[a, m, piece], z_rs.at[a, m, piece])
        return remote(zs.at[a, m, rows], zr.at[a, m, rows], *sems, to)

    def ring(a, m):
        for piece in range(PIECES):
            rows = slice(piece * (TOK // PIECES), (piece + 1) * (TOK // PIECES))
            total = zpart[a, ring_pos[a][m], rows]
            if m not in (0, 4):
                ring_copy(a, m - 1, piece).wait_recv()
                total = total + zr[a, m - 1, rows].astype(F32)
            zs[a, m, rows] = total.astype(BF16)
            ring_copy(a, m, piece).start()

    def ring_end(a, out):
        for piece in range(PIECES):
            ring_copy(a, 3, piece).wait_recv()
            ring_copy(a, 6, piece).wait_recv()
        out[...] = (zpart[a, 7] + zr[a, 3].astype(F32) + zr[a, 6].astype(F32)).astype(BF16)

    def grad_gu(lo, hi):
        def tile(i, carry):
            cols = pl.ds(pl.multiple_of(i * 256, 256), 256)
            gwgu_o[0, cols, :] = dot(rows2[0, :, cols], dpre[c], TN).astype(BF16)
            return carry

        lax.fori_loop(lo, hi, tile, 0)

    def grad_d(lo, hi):
        def tile(i, carry):
            cols = pl.ds(pl.multiple_of(i * 512, 512), 512)
            gwd_o[0, :, cols] = dot(act[c], rows2[1, :, cols], TN).astype(BF16)
            return carry

        lax.fori_loop(lo, hi, tile, 0)

    second_part(0)
    start_out(0)
    terms[...] = jnp.zeros_like(terms)
    first_part(2)
    second_part(2)
    start_out(2)
    forward_out(0)
    for pair in incoming[2:]:
        for ex in pair:
            ex["sent1"]()
    first_part(3)
    second_part(1)
    start_out(1)
    forward_out(2)
    for cp in push_out:
        cp.start()
    combine(0)
    ring(0, 0)
    ring(0, 4)
    second_part(3)
    forward_out(1)
    start_out(3)
    second_part(4)
    start_out(4)
    ring(0, 1)
    ring(0, 5)
    combine(2)
    forward_out(3)
    combine(1)
    ring(1, 0)
    ring(1, 4)
    ring(0, 2)
    forward_out(4)
    for cp in push_come:
        cp.wait_recv()
    grad_gu(0, 2)
    ring(1, 1)
    ring(0, 6)
    ring(0, 3)
    grad_gu(2, 3)
    combine(3)
    ring(1, 2)
    ring(1, 5)
    grad_gu(3, 5)
    kept = terms[...] * onehot[...]
    total = jnp.zeros((TOP, TOK), F32)
    for e in range(EXP):
        value = jnp.sum(kept[e * CAP : (e + 1) * CAP], axis=0, keepdims=True)
        total += jnp.where(local_ids == e, value, 0.0)
    for k in range(TOP):
        gsend[k] = jnp.broadcast_to(total[k : k + 1], (8, TOK))
    g_out, g_come = [], []
    for d in range(1, NZ):
        j, back = (z + d) % NZ, (z + NZ - d) % NZ
        sems = (g_ss.at[d - 1], g_rs.at[d - 1])
        g_out.append(remote(gsend.at[j], gin.at[z], *sems, dev(j, x, y, c)))
        g_come.append(remote(gsend.at[j], gin.at[back], *sems, dev(j, x, y, c)))
    for cp in g_out:
        cp.start()
    gin[z] = gsend[z]

    grad_gu(5, 8)
    arrive_out(4)
    block_sum(1, 5)
    ring(1, 6)
    block_sum(1, 6)
    ring(1, 3)
    block_sum(1, 7)
    grad_d(0, 4)
    ring_end(0, mixed_o)
    for cp in g_come:
        cp.wait_recv()
    gg_o[...] = jnp.sum(gin[...], axis=0)[:1]
    ring_end(1, gtok_o)

    for cp in w_out:
        cp.wait_send()
    for pair in incoming:
        for ex in pair:
            ex["sent2"]()
    for cp in push_out:
        cp.wait_send()
    for pair in outgoing:
        for ex in pair:
            ex["sent1"]()
            ex["sent2"]()
    for a in range(2):
        for m in range(7):
            for piece in range(PIECES):
                ring_copy(a, m, piece).wait_send()
    for cp in g_out:
        cp.wait_send()


def move(m_in, t_in, gu_in, d_in, g_in, m_out, t_out, gu_out, d_out, g_out, sems):
    copies = []
    for src, dst, pieces in (
        (gu_in.at[0], gu_out.at[0], 4),
        (d_in.at[0], d_out.at[0], 2),
        (m_in, m_out, 1),
        (t_in, t_out, 1),
        (g_in, g_out, 1),
    ):
        many = src.shape[0] // pieces
        for i in range(pieces):
            at = pl.ds(i * many, many)
            copies.append(pltpu.make_async_copy(src.at[at], dst.at[at], sems.at[len(copies)]))
    for cp in copies:
        cp.start()
    for cp in copies:
        cp.wait()


def local(tokens, expert_ids, gate_weights, grad_output, w_gate_up, w_down):
    vmem = pl.BlockSpec(memory_space=pltpu.VMEM)
    hbm = pl.BlockSpec(memory_space=pl.ANY)
    dma = pltpu.SemaphoreType.DMA
    quads = (2, NX, NY, CAP, WIDTH)
    results = pl.pallas_call(
        kernel,
        out_shape=(
            pltpu.VMEM((TOK, BLK), BF16),
            pltpu.VMEM((TOK, BLK), BF16),
            pltpu.VMEM(w_gate_up.shape, BF16),
            pltpu.VMEM(w_down.shape, BF16),
            pltpu.VMEM((1, TOK), F32),
        ),
        in_specs=[hbm, vmem, vmem, hbm, hbm, hbm],
        out_specs=(vmem,) * 5,
        scratch_shapes=[
            pltpu.VMEM((TOK, WIDTH), BF16),
            pltpu.VMEM((TOK, WIDTH), BF16),
            pltpu.VMEM((2, WIDTH, 2 * FFP), BF16),
            pltpu.VMEM((2, FFP, WIDTH), BF16),
            pltpu.VMEM(quads, BF16),
            pltpu.VMEM(quads, BF16),
            pltpu.VMEM(quads, BF16),
            pltpu.VMEM(quads, BF16),
            pltpu.VMEM(quads, BF16),
            pltpu.VMEM((2, NC * SLOTS, WIDTH), BF16),
            pltpu.VMEM((2, NC * SLOTS, FFP), BF16),
            pltpu.VMEM((2, NC * SLOTS, 2 * FFP), BF16),
            pltpu.VMEM((2, SLOTS, 2 * FFP), F32),
            pltpu.VMEM((2, SLOTS, FFP), F32),
            pltpu.VMEM((SLOTS, TOK), F32),
            pltpu.VMEM((2, TOK, SLOTS), BF16),
            pltpu.VMEM((SLOTS, TOK), F32),
            pltpu.VMEM((2, NZ, TOK, BLK), F32),
            pltpu.VMEM((2, 7, TOK, BLK), BF16),
            pltpu.VMEM((2, 7, TOK, BLK), BF16),
            pltpu.VMEM((TOP, 8, TOK), F32),
            pltpu.VMEM((NZ, 8, TOK), F32),
            dma((4,)), dma((2,)), dma((2,)),
            dma((18, 6)), dma((18, 6)), dma((18, 2)),
            dma((4,)), dma((4,)),
            dma((2, 7, PIECES)), dma((2, 7, PIECES)),
            dma((7,)), dma((7,)),
        ],
        compiler_params=pltpu.CompilerParams(
            collective_id=0, has_side_effects=True, vmem_limit_bytes=54 * 1024 * 1024
        ),
        name="moe",
    )(tokens, expert_ids.T, gate_weights.T, grad_output, w_gate_up, w_down)
    mixed, grad_tokens, grad_gu, grad_dn, gates = pl.pallas_call(
        move,
        out_shape=tuple(jax.ShapeDtypeStruct(r.shape, r.dtype) for r in results),
        in_specs=[hbm] * 5,
        out_specs=(hbm,) * 5,
        scratch_shapes=[dma((9,))],
        compiler_params=pltpu.CompilerParams(vmem_limit_bytes=2 * 1024 * 1024),
        name="move",
    )(*results)
    return mixed, grad_tokens, gates.T, grad_gu, grad_dn


def solution(mesh):
    placed = (
        P("ep", None),
        P("ep", None),
        P("ep", None),
        P("ep", None),
        P(("tp", "ep"), None, None),
        P(("tp", "ep"), None, None),
    )
    return jax.shard_map(
        local,
        mesh=mesh,
        in_specs=placed,
        out_specs=(
            P("ep", "tp"),
            P("ep", "tp"),
            P("ep", "tp"),
            P(("tp", "ep"), None, None),
            P(("tp", "ep"), None, None),
        ),
        check_vma=False,
    )
```
